32 devices in a mesh: out: 4 (over z), in: 8 (over y, x, core).
Axes of the slice: x: 2, y: 2, z: 4, core: 2. Of those that a mesh axis runs over, the one named last changes fastest.
Arguments:
- tensor: bfloat16 [1024, 1024, 1024], P('out', 'in'), may hold values from -0.0078125 to 0.0078125
- linear: bfloat16 [1024, 1024], P('out', 'in'), may hold values from -0.1875 to 0.1875
- adjoint_end: float32 [128, 1024], P(None, 'in'), may hold values from -6 to 6
- states: bfloat16 [2, 128, 1024], replicated, may hold values from -6 to 6
Outputs:
- adjoint_start: float32 [128, 1024], P(None, 'in')
The draws below stay inside these ranges and needn't reach their ends.
All inputs are finite; a program needn't handle non-finite values.
Results may differ from the reference program's by a relative error of at most 0.0045.
Values may be sent and summed in bfloat16 or wider, within the bound.
A program may use at most 128 MiB of HBM per device.

```python
import jax
import jax.numpy as jnp
from jax import lax

M = 1024
TRAJ = 128
STEPS = 2


def strengthened(values, stream_key, source, target, shards_of, factor):
    owner, partner = [(jnp.arange(values.shape[dim]) // (values.shape[dim] // shards_of)).reshape([-1 if axis == dim else 1 for axis in range(values.ndim)]) for dim in (source, target)]
    chosen = jax.random.permutation(stream_key, shards_of)[partner]
    strong = (owner == chosen) | (owner == (partner + shards_of // 2) % shards_of)
    return jnp.where(strong, factor * values, values)


def level_of(stream_key, shape, shards, low, top_value):
    gain, own = 1.0, jax.random.fold_in(stream_key, 6)
    for position, shards_of in shards:
        heights = jnp.exp(jax.random.uniform(jax.random.fold_in(own, position), (shards_of,), jnp.float32, low / len(shards), top_value / len(shards)))
        gain = gain * jnp.repeat(heights, shape[position] // shards_of).reshape([-1 if axis == position else 1 for axis in range(len(shape))])
    return gain


def noise(own_key, extent, deviation, most, pieces=(), kind=jnp.bfloat16):
    factor_of = level_of(own_key, extent, pieces, -0.22, 0.18) if pieces else 1.0
    result = jax.random.normal(own_key, extent, jnp.float32) * deviation * factor_of
    return jnp.minimum(jnp.maximum(result, -most), most).astype(kind)


def gaussian_with(stream_key, extent, scale, most, shards, heavy, kind=jnp.bfloat16):
    values = scale * jax.random.normal(stream_key, extent, jnp.float32)
    if shards:
        values = values * level_of(stream_key, extent, shards, -0.22, 0.18)
    return jnp.clip(strengthened(values, jax.random.fold_in(stream_key, 3), *heavy), -most, most).astype(kind)


def setup_inputs(seed: int = 0) -> dict:
    key_of = jax.random.split(jax.random.key(seed), 5)
    tensor = gaussian_with(key_of[0], (M, M, M), (M * M) ** -0.5, 0.0078125, ((0, 4), (1, 8)), (1, 2, 8, 2.0))
    linear = noise(key_of[1], (M, M), M ** -0.5, 0.1875, ((0, 4), (1, 8)))
    adjoint_end = noise(key_of[2], (TRAJ, M), 1.0, 6.0, ((1, 8),), jnp.float32)
    states = noise(key_of[3], (STEPS, TRAJ, M), 1.0, 6.0)
    return dict(tensor=tensor, linear=linear, adjoint_end=adjoint_end, states=states)


step_size = 0.5


def reference(tensor, linear, adjoint_end, states):
    block = M // 16
    count = M // block
    adjoint = adjoint_end
    for number in range(STEPS - 1, -1, -1):
        state = states[number]
        low = adjoint.astype(jnp.bfloat16)

        def visit(carry, index):
            first, second = carry
            start = (index * block).astype(jnp.int32)
            piece = lax.dynamic_slice_in_dim(tensor, start, block, 0).reshape(block * M, M)
            lam_rows = lax.dynamic_slice_in_dim(low, start, block, 1)
            projected = lax.dot_general(state, piece, (((1,), (1,)), ((), ())), preferred_element_type=jnp.float32)
            projected = projected.reshape(TRAJ, block, M)
            first = first + jnp.einsum("bi,bij->bj", lam_rows.astype(jnp.float32), projected.astype(jnp.float32))
            pair = (lam_rows.astype(jnp.float32)[:, :, None] * state.astype(jnp.float32)[:, None, :]).astype(jnp.bfloat16)
            second = second + jnp.dot(pair.reshape(TRAJ, block * M), piece, preferred_element_type=jnp.float32)
            return (first, second), None

        zeros = jnp.zeros((TRAJ, M), jnp.float32)
        (first, second), _ = lax.scan(visit, (zeros, zeros), jnp.arange(count, dtype=jnp.int32))
        lin = jnp.dot(low, linear, preferred_element_type=jnp.float32)
        adjoint = adjoint + step_size * (lin + first + second)
    return adjoint
```

```python
import functools

import jax
import jax.numpy as jnp
from jax import lax
from jax.experimental import pallas as pl
from jax.experimental.pallas import tpu as pltpu
from jax.sharding import PartitionSpec as P

step_size = 0.5
MESH = pl.DeviceIdType.MESH
tile_modes = 8
slots = 18


def pieces(tensor, linear, state, full_low):
    rows_block = tensor.shape[0]
    cols_block = tensor.shape[1]
    modes = tensor.shape[2]
    batch = full_low.shape[0]
    lam_rows = lax.dynamic_slice_in_dim(full_low, lax.axis_index("out") * rows_block, rows_block, 1)
    state_cols = lax.dynamic_slice_in_dim(state, lax.axis_index("in") * cols_block, cols_block, 1)
    flat = tensor.reshape(rows_block * cols_block, modes)
    projected = lax.dot_general(
        state, flat, (((1,), (1,)), ((), ())), preferred_element_type=jnp.float32
    )
    projected = projected.reshape(batch, rows_block, cols_block)
    lam_float = lam_rows.astype(jnp.float32)
    first = jnp.einsum("bi,bij->bj", lam_float, projected)
    lin = jnp.dot(lam_rows, linear, preferred_element_type=jnp.float32)
    pair = (lam_float[:, :, None] * state_cols.astype(jnp.float32)[:, None, :]).astype(jnp.bfloat16)
    second = jnp.dot(
        pair.reshape(batch, rows_block * cols_block), flat, preferred_element_type=jnp.float32
    )
    return (lin + first, second)


def plain(tensor, linear, adjoint_end, states):
    steps_total = states.shape[0]
    lam_own = adjoint_end
    for number in range(steps_total - 1, -1, -1):
        full_low = lax.all_gather(lam_own.astype(jnp.bfloat16), "in", axis=1, tiled=True)
        local, second = pieces(tensor, linear, states[number], full_low)
        second_own = lax.psum_scatter(second, "in", scatter_dimension=1, tiled=True)
        total = lax.psum(local + second_own, "out")
        lam_own = lam_own + step_size * total
    return lam_own


def kernel(n_out, n_in, rows, cols,
           flat_ref, linear_ref, adjoint_ref, states_ref, out_ref,
           tbuf, kept, st, lowsrc, lowbuf, lowf, low_t, acc, first_t,
           send1, recv1, part2, recv2, lamq, finrecv,
           tsem, s1, r1, s2, r2, ls, lr, fs, fr):
    batch = adjoint_ref.shape[0]
    quarter = batch // n_out
    ratio = rows // cols
    tiles = rows // tile_modes
    tile_rows = tile_modes * cols
    held = tbuf.shape[0]
    base = tiles - held
    o = lax.axis_index("out")
    c = lax.axis_index("in")
    plane = c // ratio
    part = lax.rem(c, ratio)

    def load(number):
        tile = lax.rem(number, tiles)
        slot = lax.rem(number, held)
        return pltpu.make_async_copy(
            flat_ref.at[pl.ds(pl.multiple_of(tile * tile_rows, tile_rows), tile_rows)],
            tbuf.at[slot], tsem.at[slot])

    @pl.loop(0, held)
    def _(number):
        load(number).start()

    barrier = pltpu.get_barrier_semaphore()
    for d in range(1, n_in):
        pl.semaphore_signal(barrier, inc=1, device_id=(o, lax.rem(c + d, n_in)), device_id_type=MESH)
    for d in range(1, n_out):
        pl.semaphore_signal(barrier, inc=1, device_id=(lax.rem(o + d, n_out), c), device_id_type=MESH)
    for q in range(n_out):
        for e in range(ratio):
            source = o * ratio + e

            @pl.when(jnp.logical_or(o != q, c != source))
            def _():
                pl.semaphore_signal(barrier, inc=1, device_id=(q, source), device_id_type=MESH)

    @pl.when(plane == o)
    def _():
        pl.semaphore_wait(barrier, 2 * n_in + n_out - 3)

    @pl.when(plane != o)
    def _():
        pl.semaphore_wait(barrier, 2 * n_in + n_out - 2)

    def low_copy(step, x):
        return pltpu.make_async_remote_copy(
            src_ref=lowsrc.at[step], dst_ref=lowbuf.at[step, part, o],
            send_sem=ls.at[step, x], recv_sem=lr.at[step, part, o],
            device_id=(plane, x), device_id_type=MESH)

    def low_start(step):
        lowsrc[step] = lamq[...].astype(jnp.bfloat16)
        for x in range(n_in):
            @pl.when(jnp.logical_or(plane != o, c != x))
            def _():
                low_copy(step, x).start()

        @pl.when(plane == o)
        def _():
            lowbuf[step, part, o] = lowsrc[step]

    def low_wait(step):
        for e in range(ratio):
            for q in range(n_out):
                @pl.when(jnp.logical_or(o != q, c != o * ratio + e))
                def _():
                    pltpu.make_async_remote_copy(
                        src_ref=lowsrc.at[step], dst_ref=lowbuf.at[step, e, q],
                        send_sem=ls.at[step, 0], recv_sem=lr.at[step, e, q],
                        device_id=(plane, c), device_id_type=MESH).wait_recv()
        for e in range(ratio):
            block = lowbuf[step, e].reshape(batch, cols).astype(jnp.float32)
            lowf[e] = block
            low_t[e * cols:(e + 1) * cols] = block.T
        for x in range(n_in):
            @pl.when(jnp.logical_or(plane != o, c != x))
            def _():
                low_copy(step, x).wait_send()

    def add_second(step, tile, slot):
        per = cols // tile_modes
        offset = lax.rem(tile, per) * tile_modes
        turned = pltpu.roll(lowf[tile // per], lax.rem(cols - offset, cols), 1)
        own = states_ref[step, :, pl.ds(pl.multiple_of(c * cols, cols), cols)].astype(jnp.float32)
        pair = jnp.concatenate(
            [(turned[:, q:q + 1] * own).astype(jnp.bfloat16) for q in range(tile_modes)], axis=1)
        acc[...] += jnp.dot(pair, tbuf[slot], preferred_element_type=jnp.float32)

    def add_first(tile, projected):
        low = low_t[pl.ds(pl.multiple_of(tile * tile_modes, tile_modes), tile_modes)]
        total = first_t[...]
        for q in range(tile_modes):
            total += low[q:q + 1] * projected[q * cols:(q + 1) * cols]
        first_t[...] = total

    def exchange(step):
        for x in range(n_in):
            send1[x] = acc[:, x * cols:(x + 1) * cols].astype(jnp.bfloat16)
        copies = []
        for d in range(1, n_in):
            target = lax.rem(c + d, n_in)
            copy = pltpu.make_async_remote_copy(
                src_ref=send1.at[target], dst_ref=recv1.at[step, d],
                send_sem=s1.at[step, d], recv_sem=r1.at[step, d],
                device_id=(o, target), device_id_type=MESH)
            copy.start()
            copies.append(copy)
        total = first_t[...].T + acc[:, pl.ds(pl.multiple_of(c * cols, cols), cols)]
        for e in range(ratio):
            total += jnp.dot(lowbuf[step, e].reshape(batch, cols), linear_ref[e * cols:(e + 1) * cols],
                             preferred_element_type=jnp.float32)
        for d in range(1, n_in):
            copies[d - 1].wait_recv()
            total += recv1[step, d].astype(jnp.float32)
        part2[...] = total.reshape(n_out, quarter, cols)
        for d in range(1, n_out):
            target = lax.rem(o + d, n_out)
            copy = pltpu.make_async_remote_copy(
                src_ref=part2.at[target], dst_ref=recv2.at[step, d],
                send_sem=s2.at[step, d], recv_sem=r2.at[step, d],
                device_id=(target, c), device_id_type=MESH)
            copy.start()
            copies.append(copy)
        mine = part2[o]
        for d in range(1, n_out):
            copies[n_in - 2 + d].wait_recv()
            mine += recv2[step, d]
        lamq[...] += step_size * mine
        return copies

    lamq[...] = adjoint_ref[pl.ds(pl.multiple_of(o * quarter, quarter), quarter)]
    low_start(1)
    st[:, :batch] = states_ref[1].T
    st[:, batch:] = states_ref[0].T
    acc[...] = jnp.zeros_like(acc)
    first_t[...] = jnp.zeros_like(first_t)
    low_wait(1)

    @pl.loop(0, tiles)
    def _(tile):
        slot = lax.rem(tile, held)
        load(tile).wait()
        both = jnp.dot(tbuf[slot], st[...], preferred_element_type=jnp.float32)
        kept[tile] = both[:, batch:]
        add_first(tile, both[:, :batch])
        add_second(1, tile, slot)

        @pl.when(tile < base)
        def _():
            load(tile + held).start()

    copies = exchange(1)
    low_start(0)
    acc[...] = jnp.zeros_like(acc)
    first_t[...] = jnp.zeros_like(first_t)
    for copy in copies:
        copy.wait_send()
    low_wait(0)

    @pl.loop(0, tiles)
    def _(visit):
        number = base + visit
        tile = lax.rem(number, tiles)
        slot = lax.rem(number, held)

        @pl.when(visit >= held)
        def _():
            load(number).wait()

        add_first(tile, kept.at[tile])
        add_second(0, tile, slot)

        @pl.when(visit < base)
        def _():
            load(number + held).start()

    copies = exchange(0)
    finals = []
    for d in range(1, n_out):
        copy = pltpu.make_async_remote_copy(
            src_ref=lamq, dst_ref=finrecv.at[d],
            send_sem=fs.at[d], recv_sem=fr.at[d],
            device_id=(lax.rem(o + d, n_out), c), device_id_type=MESH)
        copy.start()
        finals.append(copy)
    out_ref[pl.ds(pl.multiple_of(o * quarter, quarter), quarter)] = lamq[...]
    for d in range(1, n_out):
        finals[d - 1].wait_recv()
        source = lax.rem(o + n_out - d, n_out)
        out_ref[pl.ds(pl.multiple_of(source * quarter, quarter), quarter)] = finrecv[d]
    for copy in copies + finals:
        copy.wait_send()


def per_device(n_out, n_in, tensor, linear, adjoint_end, states):
    rows, cols, modes = tensor.shape
    steps, batch, _ = states.shape
    fits = (steps == 2 and cols % 128 == 0 and rows % cols == 0 and batch % 128 == 0
            and batch % (32 * n_out) == 0 and n_out > 1 and n_in > 1)
    if not fits:
        return plain(tensor, linear, adjoint_end, states)
    ratio = rows // cols
    tiles = rows // tile_modes
    held = min(slots, tiles)
    quarter = batch // n_out
    dma = pltpu.SemaphoreType.DMA
    vmem = pl.BlockSpec(memory_space=pltpu.VMEM)
    return pl.pallas_call(
        functools.partial(kernel, n_out, n_in, rows, cols),
        out_shape=jax.ShapeDtypeStruct((batch, cols), jnp.float32),
        in_specs=[pl.BlockSpec(memory_space=pl.ANY), vmem, vmem, vmem],
        out_specs=vmem,
        scratch_shapes=[
            pltpu.VMEM((held, tile_modes * cols, modes), jnp.bfloat16),
            pltpu.VMEM((tiles, tile_modes * cols, batch), jnp.float32),
            pltpu.VMEM((modes, steps * batch), jnp.bfloat16),
            pltpu.VMEM((steps, quarter, cols), jnp.bfloat16),
            pltpu.VMEM((steps, ratio, n_out, quarter, cols), jnp.bfloat16),
            pltpu.VMEM((ratio, batch, cols), jnp.float32),
            pltpu.VMEM((rows, batch), jnp.float32),
            pltpu.VMEM((batch, modes), jnp.float32),
            pltpu.VMEM((cols, batch), jnp.float32),
            pltpu.VMEM((n_in, batch, cols), jnp.bfloat16),
            pltpu.VMEM((steps, n_in, batch, cols), jnp.bfloat16),
            pltpu.VMEM((n_out, quarter, cols), jnp.float32),
            pltpu.VMEM((steps, n_out, quarter, cols), jnp.float32),
            pltpu.VMEM((quarter, cols), jnp.float32),
            pltpu.VMEM((n_out, quarter, cols), jnp.float32),
            dma((held,)),
            dma((steps, n_in)), dma((steps, n_in)),
            dma((steps, n_out)), dma((steps, n_out)),
            dma((steps, n_in)), dma((steps, ratio, n_out)),
            dma((n_out,)), dma((n_out,)),
        ],
        compiler_params=pltpu.CompilerParams(
            collective_id=0, has_side_effects=True, vmem_limit_bytes=62 * 2**20),
        cost_estimate=pl.CostEstimate(
            flops=4 * steps * batch * rows * cols * modes,
            bytes_accessed=2 * 2 * rows * cols * modes, transcendentals=0),
    )(tensor.reshape(rows * cols, modes), linear, adjoint_end, states)


def solution(mesh):
    placed = (P("out", "in", None), P("out", "in"), P(None, "in"), P())
    return jax.shard_map(
        functools.partial(per_device, mesh.shape["out"], mesh.shape["in"]),
        mesh=mesh, in_specs=placed, out_specs=P(None, "in"), check_vma=False
    )
```

```python
import functools

import jax
import jax.numpy as jnp
from jax import lax
from jax.experimental import pallas as pl
from jax.experimental.pallas import tpu as pltpu
from jax.sharding import PartitionSpec as P

step_size = 0.5
MESH = pl.DeviceIdType.MESH
tile_modes = 16
slots = 10
lead = 3
trail = 4


def pieces(tensor, linear, state, full_low):
    rows_block = tensor.shape[0]
    cols_block = tensor.shape[1]
    modes = tensor.shape[2]
    batch = full_low.shape[0]
    lam_rows = lax.dynamic_slice_in_dim(full_low, lax.axis_index("out") * rows_block, rows_block, 1)
    state_cols = lax.dynamic_slice_in_dim(state, lax.axis_index("in") * cols_block, cols_block, 1)
    flat = tensor.reshape(rows_block * cols_block, modes)
    projected = lax.dot_general(
        state, flat, (((1,), (1,)), ((), ())), preferred_element_type=jnp.float32
    )
    projected = projected.reshape(batch, rows_block, cols_block)
    lam_float = lam_rows.astype(jnp.float32)
    first = jnp.einsum("bi,bij->bj", lam_float, projected)
    lin = jnp.dot(lam_rows, linear, preferred_element_type=jnp.float32)
    pair = (lam_float[:, :, None] * state_cols.astype(jnp.float32)[:, None, :]).astype(jnp.bfloat16)
    second = jnp.dot(
        pair.reshape(batch, rows_block * cols_block), flat, preferred_element_type=jnp.float32
    )
    return (lin + first, second)


def plain(tensor, linear, adjoint_end, states):
    steps_total = states.shape[0]
    lam_own = adjoint_end
    for number in range(steps_total - 1, -1, -1):
        full_low = lax.all_gather(lam_own.astype(jnp.bfloat16), "in", axis=1, tiled=True)
        local, second = pieces(tensor, linear, states[number], full_low)
        second_own = lax.psum_scatter(second, "in", scatter_dimension=1, tiled=True)
        total = lax.psum(local + second_own, "out")
        lam_own = lam_own + step_size * total
    return lam_own


def kernel(n_out, n_in, rows, cols,
           flat_ref, linear_ref, adjoint_ref, states_ref, out_ref,
           tbuf, kept, early, st, lowsrc, lowbuf, lowf, low_t, acc, first_t,
           send1, recv1, part2, recv2, lamq, finrecv,
           tsem, s1, r1, s2, r2, ls, lr, fs, fr):
    batch = adjoint_ref.shape[0]
    quarter = batch // n_out
    ratio = rows // cols
    tiles = rows // tile_modes
    tile_rows = tile_modes * cols
    held = tbuf.shape[0]
    base = tiles - held
    begin = early.shape[0]
    end = max(tiles - trail, begin)
    o = lax.axis_index("out")
    c = lax.axis_index("in")
    plane = c // ratio
    part = lax.rem(c, ratio)

    def load(number):
        tile = lax.rem(number, tiles)
        slot = lax.rem(number, held)
        return pltpu.make_async_copy(
            flat_ref.at[pl.ds(pl.multiple_of(tile * tile_rows, tile_rows), tile_rows)],
            tbuf.at[slot], tsem.at[slot])

    @pl.loop(0, held)
    def _(number):
        load(number).start()

    barrier = pltpu.get_barrier_semaphore()
    for d in range(1, n_in):
        pl.semaphore_signal(barrier, inc=1, device_id=(o, lax.rem(c + d, n_in)), device_id_type=MESH)
    for d in range(1, n_out):
        pl.semaphore_signal(barrier, inc=1, device_id=(lax.rem(o + d, n_out), c), device_id_type=MESH)
    for q in range(n_out):
        for e in range(ratio):
            source = o * ratio + e

            @pl.when(jnp.logical_or(o != q, c != source))
            def _():
                pl.semaphore_signal(barrier, inc=1, device_id=(q, source), device_id_type=MESH)

    st[:, :batch] = states_ref[1].T
    st[:, batch:] = states_ref[0].T
    acc[...] = jnp.zeros_like(acc)
    first_t[...] = jnp.zeros_like(first_t)

    @pl.when(plane == o)
    def _():
        pl.semaphore_wait(barrier, 2 * n_in + n_out - 3)

    @pl.when(plane != o)
    def _():
        pl.semaphore_wait(barrier, 2 * n_in + n_out - 2)

    def low_copy(step, x):
        return pltpu.make_async_remote_copy(
            src_ref=lowsrc.at[step], dst_ref=lowbuf.at[step, part, o],
            send_sem=ls.at[step, x], recv_sem=lr.at[step, part, o],
            device_id=(plane, x), device_id_type=MESH)

    def low_start(step):
        lowsrc[step] = lamq[...].astype(jnp.bfloat16)
        for x in range(n_in):
            @pl.when(jnp.logical_or(plane != o, c != x))
            def _():
                low_copy(step, x).start()

        @pl.when(plane == o)
        def _():
            lowbuf[step, part, o] = lowsrc[step]

    def low_wait(step):
        for e in range(ratio):
            for q in range(n_out):
                @pl.when(jnp.logical_or(o != q, c != o * ratio + e))
                def _():
                    pltpu.make_async_remote_copy(
                        src_ref=lowsrc.at[step], dst_ref=lowbuf.at[step, e, q],
                        send_sem=ls.at[step, 0], recv_sem=lr.at[step, e, q],
                        device_id=(plane, c), device_id_type=MESH).wait_recv()
        for e in range(ratio):
            block = lowbuf[step, e].reshape(batch, cols).astype(jnp.float32)
            lowf[e] = block
            low_t[e * cols:(e + 1) * cols] = block.T
        for x in range(n_in):
            @pl.when(jnp.logical_or(plane != o, c != x))
            def _():
                low_copy(step, x).wait_send()

    def add_second(step, tile, slot):
        per = cols // tile_modes
        offset = lax.rem(tile, per) * tile_modes
        turned = pltpu.roll(lowf[tile // per], lax.rem(cols - offset, cols), 1)
        own = states_ref[step, :, pl.ds(pl.multiple_of(c * cols, cols), cols)].astype(jnp.float32)
        pair = jnp.concatenate(
            [(turned[:, q:q + 1] * own).astype(jnp.bfloat16) for q in range(tile_modes)], axis=1)
        acc[...] += jnp.dot(pair, tbuf[slot], preferred_element_type=jnp.float32)

    def add_first(tile, projected):
        low = low_t[pl.ds(pl.multiple_of(tile * tile_modes, tile_modes), tile_modes)]
        total = first_t[...]
        for q in range(tile_modes):
            total += low[q:q + 1] * projected[q * cols:(q + 1) * cols].astype(jnp.float32)
        first_t[...] = total

    def project(tile, slot):
        both = jnp.dot(tbuf[slot], st[...], preferred_element_type=jnp.float32)
        kept[tile] = both[:, batch:].astype(jnp.bfloat16)
        return both[:, :batch]

    def refill(tile):
        @pl.when(tile < base)
        def _():
            load(tile + held).start()

    def exchange(step, between):
        for x in range(n_in):
            send1[x] = acc[:, x * cols:(x + 1) * cols].astype(jnp.bfloat16)
        copies = []
        for d in range(1, n_in):
            target = lax.rem(c + d, n_in)
            copy = pltpu.make_async_remote_copy(
                src_ref=send1.at[target], dst_ref=recv1.at[step, d],
                send_sem=s1.at[step, d], recv_sem=r1.at[step, d],
                device_id=(o, target), device_id_type=MESH)
            copy.start()
            copies.append(copy)
        between()
        total = first_t[...].T + acc[:, pl.ds(pl.multiple_of(c * cols, cols), cols)]
        for e in range(ratio):
            total += jnp.dot(lowbuf[step, e].reshape(batch, cols), linear_ref[e * cols:(e + 1) * cols],
                             preferred_element_type=jnp.float32)
        for d in range(1, n_in):
            copies[d - 1].wait_recv()
            total += recv1[step, d].astype(jnp.float32)
        part2[...] = total.reshape(n_out, quarter, cols)
        for d in range(1, n_out):
            target = lax.rem(o + d, n_out)
            copy = pltpu.make_async_remote_copy(
                src_ref=part2.at[target], dst_ref=recv2.at[step, d],
                send_sem=s2.at[step, d], recv_sem=r2.at[step, d],
                device_id=(target, c), device_id_type=MESH)
            copy.start()
            copies.append(copy)
        mine = part2[o]
        for d in range(1, n_out):
            copies[n_in - 2 + d].wait_recv()
            mine += recv2[step, d]
        lamq[...] += step_size * mine
        return copies

    lamq[...] = adjoint_ref[pl.ds(pl.multiple_of(o * quarter, quarter), quarter)]
    low_start(1)

    @pl.loop(0, begin)
    def _(tile):
        load(tile).wait()
        early[tile] = project(tile, lax.rem(tile, held))

    low_wait(1)

    @pl.loop(0, begin)
    def _(tile):
        add_first(tile, early.at[tile])
        add_second(1, tile, lax.rem(tile, held))
        refill(tile)

    @pl.loop(begin, end)
    def _(tile):
        slot = lax.rem(tile, held)
        load(tile).wait()
        add_first(tile, project(tile, slot))
        add_second(1, tile, slot)
        refill(tile)

    @pl.loop(end, tiles)
    def _(tile):
        load(tile).wait()
        add_second(1, tile, lax.rem(tile, held))

    def rest_of_projection():
        @pl.loop(end, tiles)
        def _(tile):
            add_first(tile, project(tile, lax.rem(tile, held)))

    def kept_first():
        @pl.loop(0, tiles)
        def _(tile):
            add_first(tile, kept.at[tile])

    copies = exchange(1, rest_of_projection)
    low_start(0)
    acc[...] = jnp.zeros_like(acc)
    first_t[...] = jnp.zeros_like(first_t)
    for copy in copies:
        copy.wait_send()
    low_wait(0)

    @pl.loop(0, tiles)
    def _(visit):
        number = base + visit
        tile = lax.rem(number, tiles)
        slot = lax.rem(number, held)

        @pl.when(visit >= held)
        def _():
            load(number).wait()

        add_second(0, tile, slot)

        @pl.when(visit < base)
        def _():
            load(number + held).start()

    copies = exchange(0, kept_first)
    finals = []
    for d in range(1, n_out):
        copy = pltpu.make_async_remote_copy(
            src_ref=lamq, dst_ref=finrecv.at[d],
            send_sem=fs.at[d], recv_sem=fr.at[d],
            device_id=(lax.rem(o + d, n_out), c), device_id_type=MESH)
        copy.start()
        finals.append(copy)
    out_ref[pl.ds(pl.multiple_of(o * quarter, quarter), quarter)] = lamq[...]
    for d in range(1, n_out):
        finals[d - 1].wait_recv()
        source = lax.rem(o + n_out - d, n_out)
        out_ref[pl.ds(pl.multiple_of(source * quarter, quarter), quarter)] = finrecv[d]
    for copy in copies + finals:
        copy.wait_send()


def per_device(n_out, n_in, tensor, linear, adjoint_end, states):
    rows, cols, modes = tensor.shape
    steps, batch, _ = states.shape
    fits = (steps == 2 and cols % 128 == 0 and rows % cols == 0 and batch % 128 == 0
            and batch % (32 * n_out) == 0 and n_out > 1 and n_in > 1
            and rows % tile_modes == 0 and rows // tile_modes - trail >= slots - trail >= lead)
    if not fits:
        return plain(tensor, linear, adjoint_end, states)
    ratio = rows // cols
    tiles = rows // tile_modes
    held = min(slots, tiles)
    quarter = batch // n_out
    dma = pltpu.SemaphoreType.DMA
    vmem = pl.BlockSpec(memory_space=pltpu.VMEM)
    return pl.pallas_call(
        functools.partial(kernel, n_out, n_in, rows, cols),
        out_shape=jax.ShapeDtypeStruct((batch, cols), jnp.float32),
        in_specs=[pl.BlockSpec(memory_space=pl.ANY), vmem, vmem, vmem],
        out_specs=vmem,
        scratch_shapes=[
            pltpu.VMEM((held, tile_modes * cols, modes), jnp.bfloat16),
            pltpu.VMEM((tiles, tile_modes * cols, batch), jnp.bfloat16),
            pltpu.VMEM((min(lead, held), tile_modes * cols, batch), jnp.float32),
            pltpu.VMEM((modes, steps * batch), jnp.bfloat16),
            pltpu.VMEM((steps, quarter, cols), jnp.bfloat16),
            pltpu.VMEM((steps, ratio, n_out, quarter, cols), jnp.bfloat16),
            pltpu.VMEM((ratio, batch, cols), jnp.float32),
            pltpu.VMEM((rows, batch), jnp.float32),
            pltpu.VMEM((batch, modes), jnp.float32),
            pltpu.VMEM((cols, batch), jnp.float32),
            pltpu.VMEM((n_in, batch, cols), jnp.bfloat16),
            pltpu.VMEM((steps, n_in, batch, cols), jnp.bfloat16),
            pltpu.VMEM((n_out, quarter, cols), jnp.float32),
            pltpu.VMEM((steps, n_out, quarter, cols), jnp.float32),
            pltpu.VMEM((quarter, cols), jnp.float32),
            pltpu.VMEM((n_out, quarter, cols), jnp.float32),
            dma((held,)),
            dma((steps, n_in)), dma((steps, n_in)),
            dma((steps, n_out)), dma((steps, n_out)),
            dma((steps, n_in)), dma((steps, ratio, n_out)),
            dma((n_out,)), dma((n_out,)),
        ],
        compiler_params=pltpu.CompilerParams(
            collective_id=0, has_side_effects=True, vmem_limit_bytes=62 * 2**20),
        cost_estimate=pl.CostEstimate(
            flops=4 * steps * batch * rows * cols * modes,
            bytes_accessed=2 * 2 * rows * cols * modes, transcendentals=0),
    )(tensor.reshape(rows * cols, modes), linear, adjoint_end, states)


def solution(mesh):
    placed = (P("out", "in", None), P("out", "in"), P(None, "in"), P())
    return jax.shard_map(
        functools.partial(per_device, mesh.shape["out"], mesh.shape["in"]),
        mesh=mesh, in_specs=placed, out_specs=P(None, "in"), check_vma=False
    )
```

```python
import functools

import jax
import jax.numpy as jnp
from jax import lax
from jax.experimental import pallas as pl
from jax.experimental.pallas import tpu as pltpu
from jax.sharding import PartitionSpec as P

step_size = 0.5
MESH = pl.DeviceIdType.MESH
tile_modes = 16
group = 4
out_width = 256
slots = 10
lead = 3
trail = 4


def pieces(tensor, linear, state, full_low):
    rows_block = tensor.shape[0]
    cols_block = tensor.shape[1]
    modes = tensor.shape[2]
    batch = full_low.shape[0]
    lam_rows = lax.dynamic_slice_in_dim(full_low, lax.axis_index("out") * rows_block, rows_block, 1)
    state_cols = lax.dynamic_slice_in_dim(state, lax.axis_index("in") * cols_block, cols_block, 1)
    flat = tensor.reshape(rows_block * cols_block, modes)
    projected = lax.dot_general(
        state, flat, (((1,), (1,)), ((), ())), preferred_element_type=jnp.float32
    )
    projected = projected.reshape(batch, rows_block, cols_block)
    lam_float = lam_rows.astype(jnp.float32)
    first = jnp.einsum("bi,bij->bj", lam_float, projected)
    lin = jnp.dot(lam_rows, linear, preferred_element_type=jnp.float32)
    pair = (lam_float[:, :, None] * state_cols.astype(jnp.float32)[:, None, :]).astype(jnp.bfloat16)
    second = jnp.dot(
        pair.reshape(batch, rows_block * cols_block), flat, preferred_element_type=jnp.float32
    )
    return (lin + first, second)


def plain(tensor, linear, adjoint_end, states):
    steps_total = states.shape[0]
    lam_own = adjoint_end
    for number in range(steps_total - 1, -1, -1):
        full_low = lax.all_gather(lam_own.astype(jnp.bfloat16), "in", axis=1, tiled=True)
        local, second = pieces(tensor, linear, states[number], full_low)
        second_own = lax.psum_scatter(second, "in", scatter_dimension=1, tiled=True)
        total = lax.psum(local + second_own, "out")
        lam_own = lam_own + step_size * total
    return lam_own


def kernel(n_out, n_in, rows, cols,
           flat_ref, linear_ref, adjoint_ref, states_ref, out_ref,
           tbuf, kept, early, st, lowsrc, lowbuf, lowf, low_t, acc, first_t,
           send1, recv1, part2, recv2, lamq, finrecv,
           tsem, s1, r1, s2, r2, ls, lr, fs, fr):
    batch = adjoint_ref.shape[0]
    quarter = batch // n_out
    ratio = rows // cols
    tiles = rows // tile_modes
    tile_rows = tile_modes * cols
    held = tbuf.shape[0]
    base = tiles - held
    begin = early.shape[0]
    end = max(tiles - trail, begin)
    o = lax.axis_index("out")
    c = lax.axis_index("in")
    plane = c // ratio
    part = lax.rem(c, ratio)

    def load(number):
        tile = lax.rem(number, tiles)
        slot = lax.rem(number, held)
        return pltpu.make_async_copy(
            flat_ref.at[pl.ds(pl.multiple_of(tile * tile_rows, tile_rows), tile_rows)],
            tbuf.at[slot], tsem.at[slot])

    @pl.loop(0, held)
    def _(number):
        load(number).start()

    barrier = pltpu.get_barrier_semaphore()
    for d in range(1, n_in):
        pl.semaphore_signal(barrier, inc=1, device_id=(o, lax.rem(c + d, n_in)), device_id_type=MESH)
    for d in range(1, n_out):
        pl.semaphore_signal(barrier, inc=1, device_id=(lax.rem(o + d, n_out), c), device_id_type=MESH)
    for q in range(n_out):
        for e in range(ratio):
            source = o * ratio + e

            @pl.when(jnp.logical_or(o != q, c != source))
            def _():
                pl.semaphore_signal(barrier, inc=1, device_id=(q, source), device_id_type=MESH)

    st[:, :batch] = states_ref[1].T
    st[:, batch:] = states_ref[0].T
    acc[...] = jnp.zeros_like(acc)
    first_t[...] = jnp.zeros_like(first_t)

    @pl.when(plane == o)
    def _():
        pl.semaphore_wait(barrier, 2 * n_in + n_out - 3)

    @pl.when(plane != o)
    def _():
        pl.semaphore_wait(barrier, 2 * n_in + n_out - 2)

    def low_copy(step, x):
        return pltpu.make_async_remote_copy(
            src_ref=lowsrc.at[step], dst_ref=lowbuf.at[step, part, o],
            send_sem=ls.at[step, x], recv_sem=lr.at[step, part, o],
            device_id=(plane, x), device_id_type=MESH)

    def low_start(step):
        lowsrc[step] = lamq[...].astype(jnp.bfloat16)
        for x in range(n_in):
            @pl.when(jnp.logical_or(plane != o, c != x))
            def _():
                low_copy(step, x).start()

        @pl.when(plane == o)
        def _():
            lowbuf[step, part, o] = lowsrc[step]

    def low_wait(step):
        for e in range(ratio):
            for q in range(n_out):
                @pl.when(jnp.logical_or(o != q, c != o * ratio + e))
                def _():
                    pltpu.make_async_remote_copy(
                        src_ref=lowsrc.at[step], dst_ref=lowbuf.at[step, e, q],
                        send_sem=ls.at[step, 0], recv_sem=lr.at[step, e, q],
                        device_id=(plane, c), device_id_type=MESH).wait_recv()
        for e in range(ratio):
            block = lowbuf[step, e].reshape(batch, cols).astype(jnp.float32)
            lowf[e] = block
            low_t[e * cols:(e + 1) * cols] = block.T
        for x in range(n_in):
            @pl.when(jnp.logical_or(plane != o, c != x))
            def _():
                low_copy(step, x).wait_send()

    def add_second(step, tile, slot):
        per = cols // tile_modes
        offset = lax.rem(tile, per) * tile_modes
        turned = pltpu.roll(lowf[tile // per], lax.rem(cols - offset, cols), 1)
        own = states_ref[step, :, pl.ds(pl.multiple_of(c * cols, cols), cols)].astype(jnp.float32)
        pair = jnp.concatenate(
            [(turned[:, q:q + 1] * own).astype(jnp.bfloat16) for q in range(tile_modes)], axis=1)
        modes = acc.shape[1]
        width = min(out_width, modes)
        for x in range(0, modes, width):
            acc[:, x:x + width] += jnp.dot(
                pair, tbuf[slot, :, x:x + width], preferred_element_type=jnp.float32)

    def add_first(tile, projected):
        low = low_t[pl.ds(pl.multiple_of(tile * tile_modes, tile_modes), tile_modes)]
        total = first_t[...]
        for q in range(tile_modes):
            total += low[q:q + 1] * projected[q * cols:(q + 1) * cols].astype(jnp.float32)
        first_t[...] = total

    def project(tile, slot, store=None):
        if store is None:
            low = low_t[pl.ds(pl.multiple_of(tile * tile_modes, tile_modes), tile_modes)]
            total = first_t[...]
        for x in range(0, tile_modes, group):
            span = slice(x * cols, (x + group) * cols)
            both = jnp.dot(tbuf[slot, span], st[...], preferred_element_type=jnp.float32)
            kept[tile, span] = both[:, batch:].astype(jnp.bfloat16)
            if store is not None:
                store[span] = both[:, :batch]
            else:
                for q in range(group):
                    total += low[x + q:x + q + 1] * both[q * cols:(q + 1) * cols, :batch]
        if store is None:
            first_t[...] = total

    def refill(tile):
        @pl.when(tile < base)
        def _():
            load(tile + held).start()

    def exchange(step, between):
        for x in range(n_in):
            send1[x] = acc[:, x * cols:(x + 1) * cols].astype(jnp.bfloat16)
        copies = []
        for d in range(1, n_in):
            target = lax.rem(c + d, n_in)
            copy = pltpu.make_async_remote_copy(
                src_ref=send1.at[target], dst_ref=recv1.at[step, d],
                send_sem=s1.at[step, d], recv_sem=r1.at[step, d],
                device_id=(o, target), device_id_type=MESH)
            copy.start()
            copies.append(copy)
        between()
        total = first_t[...].T + acc[:, pl.ds(pl.multiple_of(c * cols, cols), cols)]
        for e in range(ratio):
            total += jnp.dot(lowbuf[step, e].reshape(batch, cols), linear_ref[e * cols:(e + 1) * cols],
                             preferred_element_type=jnp.float32)
        for d in range(1, n_in):
            copies[d - 1].wait_recv()
            total += recv1[step, d].astype(jnp.float32)
        part2[...] = total.reshape(n_out, quarter, cols)
        for d in range(1, n_out):
            target = lax.rem(o + d, n_out)
            copy = pltpu.make_async_remote_copy(
                src_ref=part2.at[target], dst_ref=recv2.at[step, d],
                send_sem=s2.at[step, d], recv_sem=r2.at[step, d],
                device_id=(target, c), device_id_type=MESH)
            copy.start()
            copies.append(copy)
        mine = part2[o]
        for d in range(1, n_out):
            copies[n_in - 2 + d].wait_recv()
            mine += recv2[step, d]
        lamq[...] += step_size * mine
        return copies

    lamq[...] = adjoint_ref[pl.ds(pl.multiple_of(o * quarter, quarter), quarter)]
    low_start(1)

    @pl.loop(0, begin)
    def _(tile):
        load(tile).wait()
        project(tile, lax.rem(tile, held), early.at[tile])

    low_wait(1)

    @pl.loop(0, begin)
    def _(tile):
        add_first(tile, early.at[tile])
        add_second(1, tile, lax.rem(tile, held))
        refill(tile)

    @pl.loop(begin, end)
    def _(tile):
        slot = lax.rem(tile, held)
        load(tile).wait()
        project(tile, slot)
        add_second(1, tile, slot)
        refill(tile)

    @pl.loop(end, tiles)
    def _(tile):
        load(tile).wait()
        add_second(1, tile, lax.rem(tile, held))

    def rest_of_projection():
        @pl.loop(end, tiles)
        def _(tile):
            project(tile, lax.rem(tile, held))

    def kept_first():
        @pl.loop(0, tiles)
        def _(tile):
            add_first(tile, kept.at[tile])

    copies = exchange(1, rest_of_projection)
    low_start(0)
    acc[...] = jnp.zeros_like(acc)
    first_t[...] = jnp.zeros_like(first_t)
    for copy in copies:
        copy.wait_send()
    low_wait(0)

    @pl.loop(0, tiles)
    def _(visit):
        number = base + visit
        tile = lax.rem(number, tiles)
        slot = lax.rem(number, held)

        @pl.when(visit >= held)
        def _():
            load(number).wait()

        add_second(0, tile, slot)

        @pl.when(visit < base)
        def _():
            load(number + held).start()

    copies = exchange(0, kept_first)
    finals = []
    for d in range(1, n_out):
        copy = pltpu.make_async_remote_copy(
            src_ref=lamq, dst_ref=finrecv.at[d],
            send_sem=fs.at[d], recv_sem=fr.at[d],
            device_id=(lax.rem(o + d, n_out), c), device_id_type=MESH)
        copy.start()
        finals.append(copy)
    out_ref[pl.ds(pl.multiple_of(o * quarter, quarter), quarter)] = lamq[...]
    for d in range(1, n_out):
        finals[d - 1].wait_recv()
        source = lax.rem(o + n_out - d, n_out)
        out_ref[pl.ds(pl.multiple_of(source * quarter, quarter), quarter)] = finrecv[d]
    for copy in copies + finals:
        copy.wait_send()


def per_device(n_out, n_in, tensor, linear, adjoint_end, states):
    rows, cols, modes = tensor.shape
    steps, batch, _ = states.shape
    fits = (steps == 2 and cols % 128 == 0 and rows % cols == 0 and batch % 128 == 0
            and batch % (32 * n_out) == 0 and n_out > 1 and n_in > 1
            and rows % tile_modes == 0 and rows // tile_modes - trail >= slots - trail >= lead)
    if not fits:
        return plain(tensor, linear, adjoint_end, states)
    ratio = rows // cols
    tiles = rows // tile_modes
    held = min(slots, tiles)
    quarter = batch // n_out
    dma = pltpu.SemaphoreType.DMA
    vmem = pl.BlockSpec(memory_space=pltpu.VMEM)
    return pl.pallas_call(
        functools.partial(kernel, n_out, n_in, rows, cols),
        out_shape=jax.ShapeDtypeStruct((batch, cols), jnp.float32),
        in_specs=[pl.BlockSpec(memory_space=pl.ANY), vmem, vmem, vmem],
        out_specs=vmem,
        scratch_shapes=[
            pltpu.VMEM((held, tile_modes * cols, modes), jnp.bfloat16),
            pltpu.VMEM((tiles, tile_modes * cols, batch), jnp.bfloat16),
            pltpu.VMEM((min(lead, held), tile_modes * cols, batch), jnp.float32),
            pltpu.VMEM((modes, steps * batch), jnp.bfloat16),
            pltpu.VMEM((steps, quarter, cols), jnp.bfloat16),
            pltpu.VMEM((steps, ratio, n_out, quarter, cols), jnp.bfloat16),
            pltpu.VMEM((ratio, batch, cols), jnp.float32),
            pltpu.VMEM((rows, batch), jnp.float32),
            pltpu.VMEM((batch, modes), jnp.float32),
            pltpu.VMEM((cols, batch), jnp.float32),
            pltpu.VMEM((n_in, batch, cols), jnp.bfloat16),
            pltpu.VMEM((steps, n_in, batch, cols), jnp.bfloat16),
            pltpu.VMEM((n_out, quarter, cols), jnp.float32),
            pltpu.VMEM((steps, n_out, quarter, cols), jnp.float32),
            pltpu.VMEM((quarter, cols), jnp.float32),
            pltpu.VMEM((n_out, quarter, cols), jnp.float32),
            dma((held,)),
            dma((steps, n_in)), dma((steps, n_in)),
            dma((steps, n_out)), dma((steps, n_out)),
            dma((steps, n_in)), dma((steps, ratio, n_out)),
            dma((n_out,)), dma((n_out,)),
        ],
        compiler_params=pltpu.CompilerParams(
            collective_id=0, has_side_effects=True, vmem_limit_bytes=62 * 2**20),
        cost_estimate=pl.CostEstimate(
            flops=4 * steps * batch * rows * cols * modes,
            bytes_accessed=2 * 2 * rows * cols * modes, transcendentals=0),
    )(tensor.reshape(rows * cols, modes), linear, adjoint_end, states)


def solution(mesh):
    placed = (P("out", "in", None), P("out", "in"), P(None, "in"), P())
    return jax.shard_map(
        functools.partial(per_device, mesh.shape["out"], mesh.shape["in"]),
        mesh=mesh, in_specs=placed, out_specs=P(None, "in"), check_vma=False
    )
```

```python
import functools

import jax
import jax.numpy as jnp
from jax import lax
from jax.experimental import pallas as pl
from jax.experimental.pallas import tpu as pltpu
from jax.sharding import PartitionSpec as P

step_size = 0.5
MESH = pl.DeviceIdType.MESH
tile_modes = 16
group = 4
out_width = 256
slots = 10
lead = 4
trail = 4


def pieces(tensor, linear, state, full_low):
    rows_block = tensor.shape[0]
    cols_block = tensor.shape[1]
    modes = tensor.shape[2]
    batch = full_low.shape[0]
    lam_rows = lax.dynamic_slice_in_dim(full_low, lax.axis_index("out") * rows_block, rows_block, 1)
    state_cols = lax.dynamic_slice_in_dim(state, lax.axis_index("in") * cols_block, cols_block, 1)
    flat = tensor.reshape(rows_block * cols_block, modes)
    projected = lax.dot_general(
        state, flat, (((1,), (1,)), ((), ())), preferred_element_type=jnp.float32
    )
    projected = projected.reshape(batch, rows_block, cols_block)
    lam_float = lam_rows.astype(jnp.float32)
    first = jnp.einsum("bi,bij->bj", lam_float, projected)
    lin = jnp.dot(lam_rows, linear, preferred_element_type=jnp.float32)
    pair = (lam_float[:, :, None] * state_cols.astype(jnp.float32)[:, None, :]).astype(jnp.bfloat16)
    second = jnp.dot(
        pair.reshape(batch, rows_block * cols_block), flat, preferred_element_type=jnp.float32
    )
    return (lin + first, second)


def plain(tensor, linear, adjoint_end, states):
    steps_total = states.shape[0]
    lam_own = adjoint_end
    for number in range(steps_total - 1, -1, -1):
        full_low = lax.all_gather(lam_own.astype(jnp.bfloat16), "in", axis=1, tiled=True)
        local, second = pieces(tensor, linear, states[number], full_low)
        second_own = lax.psum_scatter(second, "in", scatter_dimension=1, tiled=True)
        total = lax.psum(local + second_own, "out")
        lam_own = lam_own + step_size * total
    return lam_own


def kernel(n_out, n_in, rows, cols,
           flat_ref, linear_ref, adjoint_ref, states_ref, out_ref,
           tbuf, kept, early, pair_a, pair_b, st, lowsrc, lowbuf, lowf, low_t, acc, first_t,
           send1, recv1, part2, recv2, lamq, finrecv,
           tsem, s1, r1, s2, r2, ls, lr, fs, fr):
    batch = adjoint_ref.shape[0]
    quarter = batch // n_out
    ratio = rows // cols
    tiles = rows // tile_modes
    tile_rows = tile_modes * cols
    held = tbuf.shape[0]
    base = tiles - held
    begin = early.shape[0]
    end = max(tiles - trail, begin)
    o = lax.axis_index("out")
    c = lax.axis_index("in")
    plane = c // ratio
    part = lax.rem(c, ratio)

    def load(number):
        tile = lax.rem(number, tiles)
        slot = lax.rem(number, held)
        return pltpu.make_async_copy(
            flat_ref.at[pl.ds(pl.multiple_of(tile * tile_rows, tile_rows), tile_rows)],
            tbuf.at[slot], tsem.at[slot])

    @pl.loop(0, held)
    def _(number):
        load(number).start()

    barrier = pltpu.get_barrier_semaphore()
    for d in range(1, n_in):
        pl.semaphore_signal(barrier, inc=1, device_id=(o, lax.rem(c + d, n_in)), device_id_type=MESH)
    for d in range(1, n_out):
        pl.semaphore_signal(barrier, inc=1, device_id=(lax.rem(o + d, n_out), c), device_id_type=MESH)
    for q in range(n_out):
        for e in range(ratio):
            source = o * ratio + e

            @pl.when(jnp.logical_or(o != q, c != source))
            def _():
                pl.semaphore_signal(barrier, inc=1, device_id=(q, source), device_id_type=MESH)

    st[:, :batch] = states_ref[1].T
    st[:, batch:] = states_ref[0].T
    acc[...] = jnp.zeros_like(acc)
    first_t[...] = jnp.zeros_like(first_t)

    @pl.when(plane == o)
    def _():
        pl.semaphore_wait(barrier, 2 * n_in + n_out - 3)

    @pl.when(plane != o)
    def _():
        pl.semaphore_wait(barrier, 2 * n_in + n_out - 2)

    def low_copy(step, x):
        return pltpu.make_async_remote_copy(
            src_ref=lowsrc.at[step], dst_ref=lowbuf.at[step, part, o],
            send_sem=ls.at[step, x], recv_sem=lr.at[step, part, o],
            device_id=(plane, x), device_id_type=MESH)

    def low_start(step):
        lowsrc[step] = lamq[...].astype(jnp.bfloat16)
        for x in range(n_in):
            @pl.when(jnp.logical_or(plane != o, c != x))
            def _():
                low_copy(step, x).start()

        @pl.when(plane == o)
        def _():
            lowbuf[step, part, o] = lowsrc[step]

    def low_wait(step):
        for e in range(ratio):
            for q in range(n_out):
                @pl.when(jnp.logical_or(o != q, c != o * ratio + e))
                def _():
                    pltpu.make_async_remote_copy(
                        src_ref=lowsrc.at[step], dst_ref=lowbuf.at[step, e, q],
                        send_sem=ls.at[step, 0], recv_sem=lr.at[step, e, q],
                        device_id=(plane, c), device_id_type=MESH).wait_recv()
        for e in range(ratio):
            block = lowbuf[step, e].reshape(batch, cols).astype(jnp.float32)
            lowf[e] = block
            low_t[e * cols:(e + 1) * cols] = block.T
        for x in range(n_in):
            @pl.when(jnp.logical_or(plane != o, c != x))
            def _():
                low_copy(step, x).wait_send()

    def pair_of(step, tile):
        per = cols // tile_modes
        offset = lax.rem(tile, per) * tile_modes
        turned = pltpu.roll(lowf[tile // per], lax.rem(cols - offset, cols), 1)
        own = states_ref[step, :, pl.ds(pl.multiple_of(c * cols, cols), cols)].astype(jnp.float32)
        return [(turned[:, q:q + 1] * own).astype(jnp.bfloat16) for q in range(tile_modes)]

    def make_pair(step, tile, ref):
        for q, block in enumerate(pair_of(step, tile)):
            ref[:, q * cols:(q + 1) * cols] = block

    def use_pair(ref, slot):
        modes = acc.shape[1]
        width = min(out_width, modes)
        for x in range(0, modes, width):
            acc[:, x:x + width] += jnp.dot(
                ref[...], tbuf[slot, :, x:x + width], preferred_element_type=jnp.float32)

    def add_second(step, tile, slot):
        pair = jnp.concatenate(pair_of(step, tile), axis=1)
        modes = acc.shape[1]
        width = min(out_width, modes)
        for x in range(0, modes, width):
            acc[:, x:x + width] += jnp.dot(
                pair, tbuf[slot, :, x:x + width], preferred_element_type=jnp.float32)

    def second_run(step, start, stop, before, after):
        make_pair(step, lax.rem(start, tiles), pair_a)

        @pl.loop(0, (stop - start) // 2)
        def _(turn):
            number = start + 2 * turn
            before(number)
            before(number + 1)
            make_pair(step, lax.rem(number + 1, tiles), pair_b)
            use_pair(pair_a, lax.rem(number, held))
            make_pair(step, lax.rem(number + 2, tiles), pair_a)
            use_pair(pair_b, lax.rem(number + 1, held))
            after(number)
            after(number + 1)

    def add_first(tile, projected):
        low = low_t[pl.ds(pl.multiple_of(tile * tile_modes, tile_modes), tile_modes)]
        total = first_t[...]
        for q in range(tile_modes):
            total += low[q:q + 1] * projected[q * cols:(q + 1) * cols].astype(jnp.float32)
        first_t[...] = total

    def project(tile, slot, store=None):
        if store is None:
            low = low_t[pl.ds(pl.multiple_of(tile * tile_modes, tile_modes), tile_modes)]
            total = first_t[...]
        for x in range(0, tile_modes, group):
            span = slice(x * cols, (x + group) * cols)
            both = jnp.dot(tbuf[slot, span], st[...], preferred_element_type=jnp.float32)
            kept[tile, span] = both[:, batch:].astype(jnp.bfloat16)
            if store is not None:
                store[span] = both[:, :batch]
            else:
                for q in range(group):
                    total += low[x + q:x + q + 1] * both[q * cols:(q + 1) * cols, :batch]
        if store is None:
            first_t[...] = total

    def refill(tile):
        @pl.when(tile < base)
        def _():
            load(tile + held).start()

    def exchange(step, between):
        for x in range(n_in):
            send1[x] = acc[:, x * cols:(x + 1) * cols].astype(jnp.bfloat16)
        copies = []
        for d in range(1, n_in):
            target = lax.rem(c + d, n_in)
            copy = pltpu.make_async_remote_copy(
                src_ref=send1.at[target], dst_ref=recv1.at[step, d],
                send_sem=s1.at[step, d], recv_sem=r1.at[step, d],
                device_id=(o, target), device_id_type=MESH)
            copy.start()
            copies.append(copy)
        between()
        total = first_t[...].T + acc[:, pl.ds(pl.multiple_of(c * cols, cols), cols)]
        for e in range(ratio):
            total += jnp.dot(lowbuf[step, e].reshape(batch, cols), linear_ref[e * cols:(e + 1) * cols],
                             preferred_element_type=jnp.float32)
        for d in range(1, n_in):
            copies[d - 1].wait_recv()
            total += recv1[step, d].astype(jnp.float32)
        part2[...] = total.reshape(n_out, quarter, cols)
        for d in range(1, n_out):
            target = lax.rem(o + d, n_out)
            copy = pltpu.make_async_remote_copy(
                src_ref=part2.at[target], dst_ref=recv2.at[step, d],
                send_sem=s2.at[step, d], recv_sem=r2.at[step, d],
                device_id=(target, c), device_id_type=MESH)
            copy.start()
            copies.append(copy)
        mine = part2[o]
        for d in range(1, n_out):
            copies[n_in - 2 + d].wait_recv()
            mine += recv2[step, d]
        lamq[...] += step_size * mine
        return copies

    lamq[...] = adjoint_ref[pl.ds(pl.multiple_of(o * quarter, quarter), quarter)]
    low_start(1)

    @pl.loop(0, begin)
    def _(tile):
        load(tile).wait()
        project(tile, lax.rem(tile, held), early.at[tile])

    low_wait(1)

    def after_early(tile):
        add_first(tile, early.at[tile])
        refill(tile)

    second_run(1, 0, begin, lambda tile: None, after_early)

    @pl.loop(begin, end)
    def _(tile):
        slot = lax.rem(tile, held)
        load(tile).wait()
        project(tile, slot)
        add_second(1, tile, slot)
        refill(tile)

    second_run(1, end, tiles, lambda tile: load(tile).wait(), lambda tile: None)

    def rest_of_projection():
        @pl.loop(end, tiles)
        def _(tile):
            project(tile, lax.rem(tile, held))

    def kept_first():
        @pl.loop(0, tiles)
        def _(tile):
            add_first(tile, kept.at[tile])

    copies = exchange(1, rest_of_projection)
    low_start(0)
    acc[...] = jnp.zeros_like(acc)
    first_t[...] = jnp.zeros_like(first_t)
    for copy in copies:
        copy.wait_send()
    low_wait(0)

    def wait_again(number):
        @pl.when(number >= tiles)
        def _():
            load(number).wait()

    def load_again(number):
        @pl.when(number < 2 * base)
        def _():
            load(number + held).start()

    second_run(0, base, base + tiles, wait_again, load_again)

    copies = exchange(0, kept_first)
    finals = []
    for d in range(1, n_out):
        copy = pltpu.make_async_remote_copy(
            src_ref=lamq, dst_ref=finrecv.at[d],
            send_sem=fs.at[d], recv_sem=fr.at[d],
            device_id=(lax.rem(o + d, n_out), c), device_id_type=MESH)
        copy.start()
        finals.append(copy)
    out_ref[pl.ds(pl.multiple_of(o * quarter, quarter), quarter)] = lamq[...]
    for d in range(1, n_out):
        finals[d - 1].wait_recv()
        source = lax.rem(o + n_out - d, n_out)
        out_ref[pl.ds(pl.multiple_of(source * quarter, quarter), quarter)] = finrecv[d]
    for copy in copies + finals:
        copy.wait_send()


def per_device(n_out, n_in, tensor, linear, adjoint_end, states):
    rows, cols, modes = tensor.shape
    steps, batch, _ = states.shape
    fits = (steps == 2 and cols % 128 == 0 and rows % cols == 0 and batch % 128 == 0
            and batch % (32 * n_out) == 0 and n_out > 1 and n_in > 1
            and rows % tile_modes == 0 and rows // tile_modes >= slots >= lead + trail
            and rows // tile_modes % 2 == 0)
    if not fits:
        return plain(tensor, linear, adjoint_end, states)
    ratio = rows // cols
    tiles = rows // tile_modes
    held = min(slots, tiles)
    quarter = batch // n_out
    dma = pltpu.SemaphoreType.DMA
    vmem = pl.BlockSpec(memory_space=pltpu.VMEM)
    return pl.pallas_call(
        functools.partial(kernel, n_out, n_in, rows, cols),
        out_shape=jax.ShapeDtypeStruct((batch, cols), jnp.float32),
        in_specs=[pl.BlockSpec(memory_space=pl.ANY), vmem, vmem, vmem],
        out_specs=vmem,
        scratch_shapes=[
            pltpu.VMEM((held, tile_modes * cols, modes), jnp.bfloat16),
            pltpu.VMEM((tiles, tile_modes * cols, batch), jnp.bfloat16),
            pltpu.VMEM((min(lead, held), tile_modes * cols, batch), jnp.float32),
            pltpu.VMEM((batch, tile_modes * cols), jnp.bfloat16),
            pltpu.VMEM((batch, tile_modes * cols), jnp.bfloat16),
            pltpu.VMEM((modes, steps * batch), jnp.bfloat16),
            pltpu.VMEM((steps, quarter, cols), jnp.bfloat16),
            pltpu.VMEM((steps, ratio, n_out, quarter, cols), jnp.bfloat16),
            pltpu.VMEM((ratio, batch, cols), jnp.float32),
            pltpu.VMEM((rows, batch), jnp.float32),
            pltpu.VMEM((batch, modes), jnp.float32),
            pltpu.VMEM((cols, batch), jnp.float32),
            pltpu.VMEM((n_in, batch, cols), jnp.bfloat16),
            pltpu.VMEM((steps, n_in, batch, cols), jnp.bfloat16),
            pltpu.VMEM((n_out, quarter, cols), jnp.float32),
            pltpu.VMEM((steps, n_out, quarter, cols), jnp.float32),
            pltpu.VMEM((quarter, cols), jnp.float32),
            pltpu.VMEM((n_out, quarter, cols), jnp.float32),
            dma((held,)),
            dma((steps, n_in)), dma((steps, n_in)),
            dma((steps, n_out)), dma((steps, n_out)),
            dma((steps, n_in)), dma((steps, ratio, n_out)),
            dma((n_out,)), dma((n_out,)),
        ],
        compiler_params=pltpu.CompilerParams(
            collective_id=0, has_side_effects=True, vmem_limit_bytes=62 * 2**20),
        cost_estimate=pl.CostEstimate(
            flops=4 * steps * batch * rows * cols * modes,
            bytes_accessed=2 * 2 * rows * cols * modes, transcendentals=0),
    )(tensor.reshape(rows * cols, modes), linear, adjoint_end, states)


def solution(mesh):
    placed = (P("out", "in", None), P("out", "in"), P(None, "in"), P())
    return jax.shard_map(
        functools.partial(per_device, mesh.shape["out"], mesh.shape["in"]),
        mesh=mesh, in_specs=placed, out_specs=P(None, "in"), check_vma=False
    )
```
